256 devices in a mesh: ri: 8 (over z_hi, y), rj: 32 (over x, z_lo, core).
Axes of the slice: x: 4, y: 4, z: 8 (z_hi: 2, z_lo: 4; z = z_hi * 4 + z_lo), core: 2. Of those that a mesh axis runs over, the one named last changes fastest.
Arguments:
- pair_state: float32 [1024, 1024, 128], P('ri', 'rj'), may hold values from -120 to 120, as said below
- gains_in: float32 [2, 128], replicated, may hold values from 0.1 to 1.9
- edge_weight: bfloat16 [2, 128, 512], replicated, may hold values from -0.5 to 0.5
- gate_weight: bfloat16 [2, 128, 128], replicated, may hold values from -0.5 to 0.5
- gains_out: float32 [2, 128], replicated, may hold values from 0.1 to 1.9
- out_weight: bfloat16 [2, 128, 128], replicated, may hold values from -0.5 to 0.5
Outputs:
- updated: float32 [1024, 1024, 128], P('ri', 'rj')
The draws below stay inside these ranges and needn't reach their ends.
Inputs may be any that keep to these rules, and one draw needn't show every extreme that they name: `pair_state`: independent values with magnitudes that vary over residues and channels.
All inputs are finite; a program needn't handle non-finite values.
Results may differ from the reference program's by a relative error of at most 0.0012.
Values may be sent and summed in bfloat16 or wider, within the bound.
No kernel may reach another device: no remote copies, remote signals or barrier semaphores. Data moves between devices by JAX's collectives and lax.ppermute only.
A program may use at most 64 MiB of HBM per device.

```python
import math
import jax
import jax.numpy as jnp
from jax import lax

C = 128
N = 1024


def draw_pair_state(key, part):
    key = jax.random.fold_in(key, 11)
    keys = jax.random.split(key, 4)
    base = jnp.clip(jax.random.normal(keys[0], (N, N, C), jnp.float32), -6.0, 6.0)
    reach = math.log(10.0) / 2.0
    row_scale = jnp.exp(jax.random.uniform(keys[1], (N,), jnp.float32, 0.0, reach))
    col_scale = jnp.exp(jax.random.uniform(keys[2], (N,), jnp.float32, 0.0, reach))
    chan_scale = jnp.exp(jax.random.uniform(keys[3], (C,), jnp.float32, math.log(0.5), math.log(2.0)))
    return base * row_scale[:, None, None] * col_scale[None, :, None] * chan_scale[None, None, :]


def gaussian(own_key, dims, scale, limit, dtype=jnp.bfloat16):
    drawn = jax.random.normal(own_key, dims, jnp.float32) * scale
    return jnp.minimum(jnp.maximum(drawn, -limit), limit).astype(dtype)


def setup_inputs(seed: int = 0) -> dict:
    key_of = jax.random.split(jax.random.key(seed), 7)
    return {
        "pair_state": draw_pair_state(jax.random.fold_in(key_of[6], 71), 0),
        "gains_in": jnp.clip(1.0 + 0.18 * jax.random.normal(key_of[1], (2, C), jnp.float32), 0.1, 1.9),
        "edge_weight": gaussian(key_of[2], (2, C, 4 * C), C ** -0.5, 0.5),
        "gate_weight": gaussian(key_of[3], (2, C, C), C ** -0.5, 0.5),
        "gains_out": jnp.clip(1.0 + 0.18 * jax.random.normal(key_of[4], (2, C), jnp.float32), 0.1, 1.9),
        "out_weight": gaussian(key_of[5], (2, C, C), C ** -0.5, 0.5),
    }


epsilon = 1e-05

def layer_norm(values, gain):
    center = lax.optimization_barrier(jnp.mean(values, axis=-1, keepdims=True))
    spread = lax.optimization_barrier(jnp.mean(jnp.square(values - center), axis=-1, keepdims=True))
    return (values - center) * lax.rsqrt(spread + epsilon) * gain

def edges(normed, weight):

    def one_row(row_in):
        projected = jnp.dot(row_in, weight, preferred_element_type=jnp.float32)
        width = row_in.shape[-1]
        left_edge = jax.nn.sigmoid(projected[:, width:2 * width]) * projected[:, :width]
        right_edge = jax.nn.sigmoid(projected[:, 3 * width:]) * projected[:, 2 * width:3 * width]
        return (left_edge.astype(jnp.bfloat16), right_edge.astype(jnp.bfloat16))
    return lax.map(one_row, normed)

def contract(left_edge, right_edge, incoming):
    left_major = jnp.transpose(left_edge, (2, 0, 1))
    right_major = jnp.transpose(right_edge, (2, 0, 1))

    def one_channel(couple):
        left_one = couple[0].astype(jnp.float32)
        right_one = couple[1].astype(jnp.float32)
        if incoming:
            return jnp.dot(left_one.T, right_one, precision=lax.Precision.HIGHEST)
        return jnp.dot(left_one, right_one.T, precision=lax.Precision.HIGHEST)
    product = lax.map(one_channel, (left_major, right_major))
    return jnp.transpose(product, (1, 2, 0))

def update(state, gain_in, weight_edge, weight_gate, gain_out, weight_out, incoming):
    normed = layer_norm(state, gain_in).astype(jnp.bfloat16)
    left_edge, right_edge = edges(normed, weight_edge)
    product = contract(left_edge, right_edge, incoming)

    def one_row(inputs):
        normed_row, product_row, state_row = inputs
        mixed = layer_norm(product_row, gain_out).astype(jnp.bfloat16)
        gating = jax.nn.sigmoid(jnp.dot(normed_row, weight_gate, preferred_element_type=jnp.float32))
        return state_row + gating * jnp.dot(mixed, weight_out, preferred_element_type=jnp.float32)
    return lax.map(one_row, (normed, product, state))

def reference(pair_state, gains_in, edge_weight, gate_weight, gains_out, out_weight):
    first = update(pair_state, gains_in[0], edge_weight[0], gate_weight[0], gains_out[0], out_weight[0], False)
    return update(first, gains_in[1], edge_weight[1], gate_weight[1], gains_out[1], out_weight[1], True)
```

```python
import functools

import jax
import jax.numpy as jnp
from jax import lax
from jax.experimental import pallas as pl
from jax.experimental.pallas import tpu as pltpu
from jax.sharding import Mesh
from jax.sharding import PartitionSpec as P

epsilon = 1e-05
bf16 = jnp.bfloat16
f32 = jnp.float32
GROUP = 16


def norm(values, gain, axis):
    center = jnp.mean(values, axis=axis, keepdims=True)
    moved = values - center
    spread = jnp.mean(jnp.square(moved), axis=axis, keepdims=True)
    return moved * lax.rsqrt(spread + epsilon) * gain


def dot(a, b, contract):
    return lax.dot_general(a, b, ((contract[:1], contract[1:]), ((), ())), preferred_element_type=f32)


def gated(projected, width):
    left = jax.nn.sigmoid(projected[width : 2 * width]) * projected[:width]
    right = jax.nn.sigmoid(projected[3 * width :]) * projected[2 * width : 3 * width]
    return left, right


def columns_of(block_ref, count):
    return jnp.concatenate([block_ref[:, col, :] for col in range(count)], axis=0)


def edges_kernel(state_ref, gain_ref, weight_ref, out_ref):
    width = gain_ref.shape[1]
    rows, count, _ = state_ref.shape
    normed = norm(columns_of(state_ref, count), gain_ref[...], 1).astype(bf16)
    left, right = gated(dot(weight_ref[...], normed, (1, 1)), width)
    out_ref[:, 0] = left.reshape(width, count, rows).astype(bf16)
    out_ref[:, 1] = right.reshape(width, count, rows).astype(bf16)


def first_edges(state, gain, weight_t):
    rows, cols, width = state.shape
    return pl.pallas_call(
        edges_kernel,
        grid=(cols // GROUP,),
        in_specs=[
            pl.BlockSpec((rows, GROUP, width), lambda g: (0, g, 0)),
            pl.BlockSpec((1, width), lambda g: (0, 0)),
            pl.BlockSpec((4 * width, width), lambda g: (0, 0)),
        ],
        out_specs=pl.BlockSpec((width, 2, GROUP, rows), lambda g: (0, 0, g, 0)),
        out_shape=jax.ShapeDtypeStruct((width, 2, cols, rows), bf16),
        compiler_params=pltpu.CompilerParams(vmem_limit_bytes=48 << 20),
        name="first_edges",
    )(state, gain, weight_t)


def turn_kernel(state_ref, gain_ref, weight_ref, gate_ref, turned_ref):
    _, count, _ = state_ref.shape
    values = columns_of(state_ref, count)
    normed = norm(values, gain_ref[...], 1).astype(bf16)
    gate_ref[...] = jax.nn.sigmoid(dot(weight_ref[...], normed, (1, 1)))
    turned_ref[...] = values.T


def first_gate(state, gain, weight_t):
    rows, cols, width = state.shape
    step = GROUP * rows
    shape = jax.ShapeDtypeStruct((width, cols * rows), f32)
    return pl.pallas_call(
        turn_kernel,
        grid=(cols // GROUP,),
        in_specs=[
            pl.BlockSpec((rows, GROUP, width), lambda g: (0, g, 0)),
            pl.BlockSpec((1, width), lambda g: (0, 0)),
            pl.BlockSpec((width, width), lambda g: (0, 0)),
        ],
        out_specs=[pl.BlockSpec((width, step), lambda g: (0, g))] * 2,
        out_shape=[shape, shape],
        compiler_params=pltpu.CompilerParams(vmem_limit_bytes=48 << 20),
        name="first_gate",
    )(state, gain, weight_t)


def outgoing_kernel(core_ref, edge_ref, own_ref, send_ref):
    blocks, parts, _, cols, rows = edge_ref.shape
    depth = parts * cols
    mine = core_ref[0] == 0
    left = jnp.concatenate([edge_ref[b, :, 0].reshape(depth, rows) for b in range(blocks)], axis=1)
    for b in range(blocks):
        right = edge_ref[b, :, 1].reshape(depth, rows)
        partial = dot(right, left, (0, 0))
        for half in range(rows // (2 * cols)):
            at = 2 * half * cols
            even, odd = partial[at : at + cols], partial[at + cols : at + 2 * cols]
            place = b * (rows // (2 * cols)) + half
            own_ref[place] = jnp.where(mine, even, odd)
            send_ref[place] = jnp.where(mine, odd, even)


def outgoing(core, edge):
    blocks, parts, _, cols, rows = edge.shape
    shape = jax.ShapeDtypeStruct((parts, cols, blocks * rows), f32)
    return pl.pallas_call(
        outgoing_kernel,
        in_specs=[pl.BlockSpec(memory_space=pltpu.SMEM), pl.BlockSpec(memory_space=pltpu.VMEM)],
        out_specs=[pl.BlockSpec(memory_space=pltpu.VMEM)] * 2,
        out_shape=[shape, shape],
        compiler_params=pltpu.CompilerParams(vmem_limit_bytes=48 << 20),
        name="outgoing",
    )(core, edge)


def add_kernel(own_ref, other_ref, out_ref):
    blocks, _, _, rows = out_ref.shape
    for b in range(blocks):
        at = slice(b * rows, (b + 1) * rows)
        out_ref[b] = (own_ref[:, :, at] + other_ref[:, :, at]).astype(bf16)


def add_partials(own, other, blocks):
    parts, cols, total = own.shape
    return pl.pallas_call(
        add_kernel,
        in_specs=[pl.BlockSpec(memory_space=pltpu.VMEM)] * 2,
        out_specs=pl.BlockSpec(memory_space=pltpu.VMEM),
        out_shape=jax.ShapeDtypeStruct((blocks, parts, cols, total // blocks), bf16),
        compiler_params=pltpu.CompilerParams(vmem_limit_bytes=48 << 20),
        name="add_partials",
    )(own, other)


def incoming_kernel(core_ref, edge_ref, other_ref, out_ref, left_ref):
    blocks, parts, _, cols, rows = edge_ref.shape
    per = rows // (2 * cols)
    core = core_ref[0]
    for b in range(blocks):
        left_ref[core, b] = edge_ref[b, :, 0]
        left_ref[1 - core, b] = other_ref[b]
    right = jnp.concatenate([edge_ref[b, :, 1].reshape(parts * cols, rows) for b in range(blocks)], axis=1)
    for place in range(blocks):
        left = jnp.concatenate(
            [
                jnp.concatenate([left_ref[side, b, place * per + half] for b in range(blocks)], axis=1)
                for half in range(per)
                for side in range(2)
            ],
            axis=0,
        )
        product = dot(right, left, (1, 1))
        out_ref[place] = product.reshape(parts, cols, rows).astype(bf16)


def incoming(core, edge, other):
    blocks, parts, _, cols, rows = edge.shape
    return pl.pallas_call(
        incoming_kernel,
        in_specs=[
            pl.BlockSpec(memory_space=pltpu.SMEM),
            pl.BlockSpec(memory_space=pltpu.VMEM),
            pl.BlockSpec(memory_space=pltpu.VMEM),
        ],
        out_specs=pl.BlockSpec(memory_space=pltpu.VMEM),
        out_shape=jax.ShapeDtypeStruct((blocks, parts, cols, rows), bf16),
        scratch_shapes=[pltpu.VMEM((2, blocks, parts, cols, rows), bf16)],
        compiler_params=pltpu.CompilerParams(vmem_limit_bytes=48 << 20),
        name="incoming",
    )(core, edge, other)


def middle_kernel(
    product_ref, gate_ref, state_ref, gain_out_ref, weight_out_ref, gain_in_ref, weight_edge_ref,
    edge_ref, next_ref, normed_ref,
):
    width, count, rows = product_ref.shape
    product = product_ref[...].astype(f32).reshape(width, count * rows)
    mixed = norm(product, gain_out_ref[...], 0).astype(bf16)
    state = state_ref[...] + gate_ref[...] * dot(weight_out_ref[...], mixed, (1, 0))
    next_ref[...] = state
    normed = norm(state, gain_in_ref[...], 0).astype(bf16)
    normed_ref[...] = normed
    left, right = gated(dot(weight_edge_ref[...], normed, (1, 0)), width)
    edge_ref[:, 0] = left.reshape(width, count, rows).astype(bf16)
    edge_ref[:, 1] = right.reshape(width, count, rows).astype(bf16)


def middle(product, gate, state, gain_out, weight_out_t, gain_in, weight_edge_t):
    width, cols, rows = product.shape
    step = GROUP * rows
    flat = pl.BlockSpec((width, step), lambda g: (0, g))
    gain = pl.BlockSpec((width, 1), lambda g: (0, 0))
    return pl.pallas_call(
        middle_kernel,
        grid=(cols // GROUP,),
        in_specs=[
            pl.BlockSpec((width, GROUP, rows), lambda g: (0, g, 0)),
            flat,
            flat,
            gain,
            pl.BlockSpec((width, width), lambda g: (0, 0)),
            gain,
            pl.BlockSpec((4 * width, width), lambda g: (0, 0)),
        ],
        out_specs=[pl.BlockSpec((width, 2, GROUP, rows), lambda g: (0, 0, g, 0)), flat, flat],
        out_shape=[
            jax.ShapeDtypeStruct((width, 2, cols, rows), bf16),
            jax.ShapeDtypeStruct((width, cols * rows), f32),
            jax.ShapeDtypeStruct((width, cols * rows), bf16),
        ],
        compiler_params=pltpu.CompilerParams(vmem_limit_bytes=56 << 20),
        name="middle",
    )(product, gate, state, gain_out, weight_out_t, gain_in, weight_edge_t)


def back_kernel(state_ref, normed_ref, weight_ref, gate_ref, turned_ref):
    gate_ref[...] = jax.nn.sigmoid(dot(normed_ref[...], weight_ref[...], (0, 0)))
    turned_ref[...] = state_ref[...].T


def second_gate(state, normed, weight, rows):
    width, pairs = state.shape
    step = GROUP * rows
    shape = jax.ShapeDtypeStruct((pairs, width), f32)
    return pl.pallas_call(
        back_kernel,
        grid=(pairs // step,),
        in_specs=[
            pl.BlockSpec((width, step), lambda g: (0, g)),
            pl.BlockSpec((width, step), lambda g: (0, g)),
            pl.BlockSpec((width, width), lambda g: (0, 0)),
        ],
        out_specs=[pl.BlockSpec((step, width), lambda g: (g, 0))] * 2,
        out_shape=[shape, shape],
        compiler_params=pltpu.CompilerParams(vmem_limit_bytes=48 << 20),
        name="second_gate",
    )(state, normed, weight)


def last_kernel(product_ref, gate_ref, state_ref, gain_ref, weight_ref, out_ref):
    width, count, rows = product_ref.shape
    product = product_ref[...].astype(f32).reshape(width, count * rows)
    mixed = norm(product, gain_ref[...], 0).astype(bf16)
    done = state_ref[...] + gate_ref[...] * dot(mixed, weight_ref[...], (0, 0))
    for col in range(count):
        out_ref[:, col, :] = done[col * rows : (col + 1) * rows]


def last(product, gate, state, gain, weight):
    width, cols, rows = product.shape
    step = GROUP * rows
    flat = pl.BlockSpec((step, width), lambda g: (g, 0))
    return pl.pallas_call(
        last_kernel,
        grid=(cols // GROUP,),
        in_specs=[
            pl.BlockSpec((width, GROUP, rows), lambda g: (0, g, 0)),
            flat,
            flat,
            pl.BlockSpec((width, 1), lambda g: (0, 0)),
            pl.BlockSpec((width, width), lambda g: (0, 0)),
        ],
        out_specs=pl.BlockSpec((rows, GROUP, width), lambda g: (0, g, 0)),
        out_shape=jax.ShapeDtypeStruct((rows, cols, width), f32),
        compiler_params=pltpu.CompilerParams(vmem_limit_bytes=48 << 20),
        name="last",
    )(product, gate, state, gain, weight)


chips = ("ri", "rp")


def exchange(values):
    return lax.all_to_all(values, chips, 0, 0, tiled=True)


def swap(values):
    return lax.ppermute(values, "core", [(0, 1), (1, 0)])


def shards(blocks, parts, state, gains_in, edge_weight, gate_weight, gains_out, out_weight):
    rows, cols, width = state.shape
    core = lax.axis_index("core").astype(jnp.int32).reshape(1)

    edge = exchange(first_edges(state, gains_in[:1], edge_weight[0].T).reshape(width, 2 * cols, rows))
    gate, turned = first_gate(state, gains_in[:1], gate_weight[0].T)
    own, send = outgoing(core, edge.reshape(blocks, parts, 2, cols, rows))
    product = add_partials(own, swap(send), blocks)
    product = exchange(product.reshape(width, cols, rows))

    edge, state, normed = middle(
        product, gate, turned, gains_out[0][:, None], out_weight[0].T, gains_in[1][:, None], edge_weight[1].T
    )
    edge = exchange(edge.reshape(width, 2 * cols, rows)).reshape(blocks, parts, 2, cols, rows)
    gate, turned = second_gate(state, normed, gate_weight[1], rows)
    product = incoming(core, edge, swap(edge[:, :, 0]))
    product = exchange(product.reshape(width, cols, rows))
    return last(product, gate, turned, gains_out[1][:, None], out_weight[1])


def solution(mesh):
    blocks, lanes = mesh.devices.shape
    mesh = Mesh(mesh.devices.reshape(blocks, lanes // 2, 2), ("ri", "rp", "core"))
    placed = P("ri", ("rp", "core"), None)
    return jax.shard_map(
        functools.partial(shards, blocks, lanes // 2),
        mesh=mesh,
        in_specs=(placed, P(), P(), P(), P(), P()),
        out_specs=placed,
        check_vma=False,
    )
```

```python
import jax
import jax.numpy as jnp
from jax import lax
from jax.experimental import pallas as pl
from jax.experimental.pallas import tpu as pltpu
from jax.sharding import Mesh
from jax.sharding import PartitionSpec as P

epsilon = 1e-05
bf16 = jnp.bfloat16
f32 = jnp.float32
GROUP = 16
SUB = 4


def norm(values, gain, axis):
    center = jnp.mean(values, axis=axis, keepdims=True)
    moved = values - center
    spread = jnp.mean(jnp.square(moved), axis=axis, keepdims=True)
    return moved * lax.rsqrt(spread + epsilon) * gain


def dot(a, b, contract):
    return lax.dot_general(a, b, ((contract[:1], contract[1:]), ((), ())), preferred_element_type=f32)


def sigmoid(values):
    return 0.5 * jnp.tanh(0.5 * values) + 0.5


def upright(row):
    return jnp.broadcast_to(row, (row.shape[1], row.shape[1])).T[:, :1]


def gated(projected, width):
    left = sigmoid(projected[width : 2 * width]) * projected[:width]
    right = sigmoid(projected[3 * width :]) * projected[2 * width : 3 * width]
    return left, right


def put_edges(out_ref, at, lefts, rights):
    width, _, _, rows = out_ref.shape
    for side, parts in enumerate((lefts, rights)):
        values = jnp.concatenate(parts, axis=1)
        out_ref[:, side, at : at + GROUP] = values.reshape(width, GROUP, rows).astype(bf16)


VMEM = pl.BlockSpec(memory_space=pltpu.VMEM)
SMEM = pl.BlockSpec(memory_space=pltpu.SMEM)
HBM = pl.BlockSpec(memory_space=pltpu.HBM)
ANY = pl.BlockSpec(memory_space=pl.ANY)


def call(kernel, name, specs, outs, shapes, scratch=(), mib=16):
    return pl.pallas_call(
        kernel,
        in_specs=specs,
        out_specs=outs,
        out_shape=shapes,
        scratch_shapes=scratch,
        compiler_params=pltpu.CompilerParams(vmem_limit_bytes=mib << 20),
        name=name,
    )


def in_hbm(*values):
    return [pltpu.with_memory_space_constraint(value, pltpu.HBM) for value in values]


def start_all(copies):
    for copy in copies:
        copy.start()


def first_edges(state, gains, weight):
    rows, cols, width = state.shape
    chunk = 8

    def kernel(state_ref, gain_hbm, weight_hbm, out_ref, held, gain_ref, weight_ref, sems):
        whole = [
            pltpu.make_async_copy(gain_hbm, gain_ref, sems.at[0]),
            pltpu.make_async_copy(weight_hbm.at[0], weight_ref, sems.at[1]),
        ]
        parts = []
        for n in range(cols // chunk):
            at = slice(n * chunk, (n + 1) * chunk)
            parts.append(pltpu.make_async_copy(state_ref.at[:, at], held.at[:, at], sems.at[2 + n]))
        start_all(parts[:1] + whole + parts[1:])
        for copy in whole:
            copy.wait()
        for at in range(0, cols, GROUP):
            lefts, rights = [], []
            for col in range(at, at + GROUP, SUB):
                if col % chunk == 0:
                    parts[col // chunk].wait()
                values = jnp.concatenate([held[:, col + s, :] for s in range(SUB)], axis=0)
                normed = norm(values, gain_ref[:1], 1).astype(bf16)
                left, right = gated(dot(weight_ref[...], normed, (0, 1)), width)
                lefts.append(left)
                rights.append(right)
            put_edges(out_ref, at, lefts, rights)

    shape = jax.ShapeDtypeStruct((width, 2, cols, rows), bf16)
    scratch = [
        pltpu.VMEM((rows, cols, width), f32),
        pltpu.VMEM(gains.shape, f32),
        pltpu.VMEM(weight.shape[1:], bf16),
        pltpu.SemaphoreType.DMA((2 + cols // chunk,)),
    ]
    return call(kernel, "first_edges", [HBM] * 3, VMEM, shape, scratch)(*in_hbm(state, gains, weight))


def first_gate(state, gains, weight):
    rows, cols, width = state.shape

    def kernel(state_ref, gain_ref, weight_ref, gate_ref, turned_ref):
        for col in range(0, cols, SUB):
            values = jnp.concatenate([state_ref[:, col + s, :] for s in range(SUB)], axis=0)
            normed = norm(values, gain_ref[:1], 1).astype(bf16)
            at = slice(col * rows, (col + SUB) * rows)
            gate_ref[:, at] = sigmoid(dot(weight_ref[0], normed, (0, 1)))
            turned_ref[:, at] = values.T

    shapes = [jax.ShapeDtypeStruct((width, cols * rows), f32)] * 2
    return call(kernel, "first_gate", [VMEM] * 3, [VMEM] * 2, shapes)(state, gains, weight)


def place_of(column_block):
    return column_block % Z_LO * X + column_block // Z_LO


def block_of(spot):
    return spot % Z_HI * Y + spot // Z_HI


def outgoing(core, edge):
    places, spots, _, cols, rows = edge.shape
    depth = places * cols
    per = rows // (2 * cols)

    def kernel(core_ref, edge_ref, own_ref, send_ref):
        mine = core_ref[0] == 0
        left = jnp.concatenate([edge_ref[:, spot, 0].reshape(depth, rows) for spot in range(spots)], axis=1)
        for spot in range(spots):
            right = edge_ref[:, spot, 1].reshape(depth, rows)
            partial = dot(right, left, (0, 0))
            for half in range(per):
                at = 2 * half * cols
                even, odd = partial[at : at + cols], partial[at + cols : at + 2 * cols]
                place = place_of(block_of(spot) * per + half)
                own_ref[place] = jnp.where(mine, even, odd)
                send_ref[place] = jnp.where(mine, odd, even)

    shapes = [jax.ShapeDtypeStruct((places, cols, spots * rows), f32)] * 2
    return call(kernel, "outgoing", [SMEM, VMEM], [VMEM] * 2, shapes)(core, edge)


def add_partials(own, other, spots, *made):
    places, cols, total = own.shape
    rows = total // spots

    def kernel(own_ref, other_ref, *refs):
        for spot in range(spots):
            at = slice(spot * rows, (spot + 1) * rows)
            refs[-1][:, spot] = (own_ref[:, :, at] + other_ref[:, :, at]).astype(bf16)

    shape = jax.ShapeDtypeStruct((places, spots, cols, rows), bf16)
    return call(kernel, "add_partials", [VMEM] * 2 + [ANY] * len(made), VMEM, shape)(own, other, *made)


def incoming(core, edge, other, *made):
    places, spots, _, cols, rows = edge.shape
    per = rows // (2 * cols)

    def kernel(core_ref, edge_ref, other_ref, *refs):
        out_ref, left_ref = refs[-2:]
        core = core_ref[0]
        for spot in range(spots):
            left_ref[core, :, spot] = edge_ref[:, spot, 0]
            left_ref[1 - core, :, spot] = other_ref[:, spot]
        right = jnp.concatenate([edge_ref[:, spot, 1].reshape(places * cols, rows) for spot in range(spots)], axis=1)
        for spot in range(spots):
            block = block_of(spot)
            left = jnp.concatenate(
                [
                    jnp.concatenate([left_ref[side, place_of(block * per + half), s] for s in range(spots)], axis=1)
                    for half in range(per)
                    for side in range(2)
                ],
                axis=0,
            )
            out_ref[:, spot] = dot(right, left, (1, 1)).reshape(places, cols, rows).astype(bf16)

    shape = jax.ShapeDtypeStruct((places, spots, cols, rows), bf16)
    scratch = [pltpu.VMEM((2,) + shape.shape, bf16)]
    specs = [SMEM, VMEM, VMEM] + [ANY] * len(made)
    return call(kernel, "incoming", specs, VMEM, shape, scratch)(core, edge, other, *made)


def middle(product, gate, state, gains_out, weight_out, gains_in, weight_edge):
    width, cols, rows = product.shape

    def kernel(
        product_ref, gate_ref, state_ref, gain_out_ref, weight_out_ref, gain_in_ref, weight_edge_ref,
        edge_ref, next_ref, normed_ref,
    ):
        gain_out, gain_in = upright(gain_out_ref[:1]), upright(gain_in_ref[1:])
        for first in range(0, cols, GROUP):
            values = product_ref[:, first : first + GROUP].astype(f32).reshape(width, GROUP * rows)
            lefts, rights = [], []
            for step in range(0, GROUP, SUB):
                at = slice((first + step) * rows, (first + step + SUB) * rows)
                product = values[:, step * rows : (step + SUB) * rows]
                mixed = norm(product, gain_out, 0).astype(bf16)
                state = state_ref[:, at] + gate_ref[:, at] * dot(weight_out_ref[0], mixed, (0, 0))
                next_ref[:, at] = state
                normed = norm(state, gain_in, 0).astype(bf16)
                normed_ref[:, at] = normed
                left, right = gated(dot(weight_edge_ref[1], normed, (0, 0)), width)
                lefts.append(left)
                rights.append(right)
            put_edges(edge_ref, first, lefts, rights)

    shapes = [
        jax.ShapeDtypeStruct((width, 2, cols, rows), bf16),
        jax.ShapeDtypeStruct((width, cols * rows), f32),
        jax.ShapeDtypeStruct((width, cols * rows), bf16),
    ]
    return call(kernel, "middle", [VMEM] * 7, [VMEM] * 3, shapes)(
        product, gate, state, gains_out, weight_out, gains_in, weight_edge
    )


def second_gate(state, normed, weight, rows):
    width, pairs = state.shape

    def kernel(state_ref, normed_ref, weight_ref, gate_ref, turned_ref):
        for start in range(0, pairs, SUB * rows):
            at = slice(start, start + SUB * rows)
            gate_ref[at] = sigmoid(dot(normed_ref[:, at], weight_ref[1], (0, 0)))
            turned_ref[at] = state_ref[:, at].T

    shapes = [jax.ShapeDtypeStruct((pairs, width), f32)] * 2
    return call(kernel, "second_gate", [VMEM] * 3, [VMEM] * 2, shapes)(state, normed, weight)


def last(product, gate, state, gains, weight):
    width, cols, rows = product.shape
    chunk = 8

    def kernel(product_ref, gate_ref, state_ref, gain_ref, weight_ref, out_ref, held, sems):
        gain = upright(gain_ref[1:])
        written = []
        for first in range(0, cols, GROUP):
            values = product_ref[:, first : first + GROUP].astype(f32).reshape(width, GROUP * rows)
            for col in range(first, first + GROUP, SUB):
                at = slice(col * rows, (col + SUB) * rows)
                mixed = norm(values[:, (col - first) * rows : (col - first + SUB) * rows], gain, 0).astype(bf16)
                done = state_ref[at] + gate_ref[at] * dot(mixed, weight_ref[1], (0, 0))
                for s in range(SUB):
                    held[:, col + s, :] = done[s * rows : (s + 1) * rows]
                if (col + SUB) % chunk == 0:
                    ready = slice(col + SUB - chunk, col + SUB)
                    written.append(pltpu.make_async_copy(held.at[:, ready], out_ref.at[:, ready], sems.at[len(written)]))
                    written[-1].start()
        for copy in written:
            copy.wait()

    shape = (rows, cols, width)
    scratch = [pltpu.VMEM(shape, f32), pltpu.SemaphoreType.DMA((cols // chunk,))]
    return call(kernel, "last", [VMEM] * 5, HBM, pltpu.HBM(shape, f32), scratch)(product, gate, state, gains, weight)


chips = ("z_lo", "x", "y", "z_hi")
X, Y, Z_HI, Z_LO = 4, 4, 2, 4


def exchange(values):
    return lax.all_to_all(values, chips, 0, 0, tiled=True)


def swap(values):
    return lax.ppermute(values, "core", [(0, 1), (1, 0)])


def shards(state, gains_in, edge_weight, gate_weight, gains_out, out_weight):
    rows, cols, width = state.shape
    by_device = (X * Z_LO, Y * Z_HI, 2, cols, rows)
    core, gains_in = lax.optimization_barrier((lax.axis_index("core").astype(jnp.int32).reshape(1), gains_in))

    edge = exchange(first_edges(state, gains_in, edge_weight).reshape(width, 2 * cols, rows))
    own, send = outgoing(core, edge.reshape(by_device))
    sent = swap(send)
    gate, turned = first_gate(state, gains_in, gate_weight)
    product = add_partials(own, sent, Y * Z_HI, gate, turned)
    product = exchange(product.reshape(width, cols, rows))

    edge, state, normed = middle(product, gate, turned, gains_out, out_weight, gains_in, edge_weight)
    edge = exchange(edge.reshape(width, 2 * cols, rows)).reshape(by_device)
    sent = swap(edge[:, :, 0])
    gate, turned = second_gate(state, normed, gate_weight, rows)
    product = incoming(core, edge, sent, gate, turned)
    product = exchange(product.reshape(width, cols, rows))
    return last(product, gate, turned, gains_out, out_weight)


def solution(mesh):
    mesh = Mesh(mesh.devices.reshape(Z_HI, Y, X, Z_LO, 2), ("z_hi", "y", "x", "z_lo", "core"))
    placed = P(("z_hi", "y"), ("x", "z_lo", "core"), None)
    return jax.shard_map(
        shards,
        mesh=mesh,
        in_specs=(placed, P(), P(), P(), P(), P()),
        out_specs=placed,
        check_vma=False,
    )
```

```python
import jax
import jax.numpy as jnp
from jax import lax
from jax.experimental import pallas as pl
from jax.experimental.pallas import tpu as pltpu
from jax.sharding import Mesh
from jax.sharding import PartitionSpec as P

epsilon = 1e-05
bf16 = jnp.bfloat16
f32 = jnp.float32
GROUP = 16
SUB = 8


def norm(values, gain, axis):
    center = jnp.mean(values, axis=axis, keepdims=True)
    moved = values - center
    spread = jnp.mean(jnp.square(moved), axis=axis, keepdims=True)
    return moved * lax.rsqrt(spread + epsilon) * gain


def dot(a, b, contract):
    return lax.dot_general(a, b, ((contract[:1], contract[1:]), ((), ())), preferred_element_type=f32)


def sigmoid(values):
    return 0.5 * jnp.tanh(0.5 * values) + 0.5


def upright(row):
    return jnp.broadcast_to(row, (row.shape[1], row.shape[1])).T[:, :1]


def halved(weight):
    return (weight.astype(f32) * 0.5).T.astype(bf16)


def gated(projected, width):
    sides = [projected[n * width : (n + 1) * width] for n in range(4)]
    return jnp.tanh(sides[1]) * sides[0] + sides[0], jnp.tanh(sides[3]) * sides[2] + sides[2]


def put_edges(out_ref, at, lefts, rights):
    width, _, _, rows = out_ref.shape
    for side, parts in enumerate((lefts, rights)):
        values = jnp.concatenate(parts, axis=1)
        out_ref[:, side, at : at + GROUP] = values.reshape(width, GROUP, rows).astype(bf16)


VMEM = pl.BlockSpec(memory_space=pltpu.VMEM)
SMEM = pl.BlockSpec(memory_space=pltpu.SMEM)
HBM = pl.BlockSpec(memory_space=pltpu.HBM)
ANY = pl.BlockSpec(memory_space=pl.ANY)


def call(kernel, name, specs, outs, shapes, scratch=(), mib=16):
    return pl.pallas_call(
        kernel,
        in_specs=specs,
        out_specs=outs,
        out_shape=shapes,
        scratch_shapes=scratch,
        compiler_params=pltpu.CompilerParams(vmem_limit_bytes=mib << 20),
        name=name,
    )


def in_hbm(*values):
    return [pltpu.with_memory_space_constraint(value, pltpu.HBM) for value in values]


def start_all(copies):
    for copy in copies:
        copy.start()


def first_edges(state, gains, weight):
    rows, cols, width = state.shape
    chunk = 8

    def kernel(state_ref, gain_hbm, weight_hbm, out_ref, held, gain_ref, weight_ref, sems):
        whole = [
            pltpu.make_async_copy(gain_hbm, gain_ref, sems.at[0]),
            pltpu.make_async_copy(weight_hbm.at[0], weight_ref, sems.at[1]),
        ]
        parts = []
        for n in range(cols // chunk):
            at = slice(n * chunk, (n + 1) * chunk)
            parts.append(pltpu.make_async_copy(state_ref.at[:, at], held.at[:, at], sems.at[2 + n]))
        start_all(parts[:1] + whole + parts[1:])
        for copy in whole:
            copy.wait()
        turned = halved(weight_ref[...])
        for at in range(0, cols, GROUP):
            lefts, rights = [], []
            for col in range(at, at + GROUP, SUB):
                if col % chunk == 0:
                    parts[col // chunk].wait()
                values = jnp.swapaxes(held[:, col : col + SUB], 0, 1).reshape(SUB * rows, width)
                normed = norm(values, gain_ref[:1], 1).astype(bf16)
                left, right = gated(dot(turned, normed, (1, 1)), width)
                lefts.append(left)
                rights.append(right)
            put_edges(out_ref, at, lefts, rights)

    shape = jax.ShapeDtypeStruct((width, 2, cols, rows), bf16)
    scratch = [
        pltpu.VMEM((rows, cols, width), f32),
        pltpu.VMEM(gains.shape, f32),
        pltpu.VMEM(weight.shape[1:], bf16),
        pltpu.SemaphoreType.DMA((2 + cols // chunk,)),
    ]
    return call(kernel, "first_edges", [HBM] * 3, VMEM, shape, scratch)(*in_hbm(state, gains, weight))


def first_gate(state, gains, weight):
    rows, cols, width = state.shape

    def kernel(state_ref, gain_ref, weight_ref, gate_ref, turned_ref):
        for col in range(0, cols, SUB):
            values = jnp.swapaxes(state_ref[:, col : col + SUB], 0, 1).reshape(SUB * rows, width)
            normed = norm(values, gain_ref[:1], 1).astype(bf16)
            at = slice(col * rows, (col + SUB) * rows)
            gate_ref[:, at] = sigmoid(dot(weight_ref[0], normed, (0, 1)))
            turned_ref[:, at] = values.T

    shapes = [jax.ShapeDtypeStruct((width, cols * rows), f32)] * 2
    return call(kernel, "first_gate", [VMEM] * 3, [VMEM] * 2, shapes)(state, gains, weight)


def place_of(column_block):
    return column_block % Z_LO * X + column_block // Z_LO


def block_of(spot):
    return spot % Z_HI * Y + spot // Z_HI


def outgoing(core, edge):
    places, spots, _, cols, rows = edge.shape
    depth = places * cols
    per = rows // (2 * cols)

    def kernel(core_ref, edge_ref, own_ref, send_ref):
        mine = core_ref[0] == 0
        left = jnp.concatenate([edge_ref[:, spot, 0].reshape(depth, rows) for spot in range(spots)], axis=1)
        for spot in range(spots):
            right = edge_ref[:, spot, 1].reshape(depth, rows)
            partial = dot(right, left, (0, 0))
            for half in range(per):
                at = 2 * half * cols
                even, odd = partial[at : at + cols], partial[at + cols : at + 2 * cols]
                place = place_of(block_of(spot) * per + half)
                own_ref[place] = jnp.where(mine, even, odd)
                send_ref[place] = jnp.where(mine, odd, even)

    shapes = [jax.ShapeDtypeStruct((places, cols, spots * rows), f32)] * 2
    return call(kernel, "outgoing", [SMEM, VMEM], [VMEM] * 2, shapes)(core, edge)


def add_partials(own, other, spots, *made):
    places, cols, total = own.shape
    rows = total // spots

    def kernel(own_ref, other_ref, *refs):
        for spot in range(spots):
            at = slice(spot * rows, (spot + 1) * rows)
            refs[-1][:, spot] = (own_ref[:, :, at] + other_ref[:, :, at]).astype(bf16)

    shape = jax.ShapeDtypeStruct((places, spots, cols, rows), bf16)
    return call(kernel, "add_partials", [VMEM] * 2 + [ANY] * len(made), VMEM, shape)(own, other, *made)


def incoming(core, edge, other, *made):
    places, spots, _, cols, rows = edge.shape
    per = rows // (2 * cols)
    pair = 2

    def kernel(core_ref, edge_ref, other_ref, *refs):
        out_ref = refs[-1]
        mine = core_ref[0] == 0

        def left_of(place, side):
            parts = []
            for spot in range(spots):
                own, fetched = edge_ref[place, spot, 0], other_ref[place, spot]
                parts.append(jnp.where(mine, fetched, own) if side else jnp.where(mine, own, fetched))
            return jnp.concatenate(parts, axis=1)

        right = jnp.concatenate([edge_ref[:, spot, 1].reshape(places * cols, rows) for spot in range(spots)], axis=1)
        for first in range(0, spots, pair):
            left = jnp.concatenate(
                [
                    left_of(place_of(block_of(spot) * per + half), side)
                    for spot in range(first, first + pair)
                    for half in range(per)
                    for side in range(2)
                ],
                axis=0,
            )
            product = dot(right, left, (1, 1))
            for n in range(pair):
                at = slice(n * rows, (n + 1) * rows)
                out_ref[:, first + n] = product[:, at].reshape(places, cols, rows).astype(bf16)

    shape = jax.ShapeDtypeStruct((places, spots, cols, rows), bf16)
    specs = [SMEM, VMEM, VMEM] + [ANY] * len(made)
    return call(kernel, "incoming", specs, VMEM, shape)(core, edge, other, *made)


def middle(product, gate, state, gains_out, weight_out, gains_in, weight_edge):
    width, cols, rows = product.shape

    def kernel(
        product_ref, gate_ref, state_ref, gain_out_ref, weight_out_ref, gain_in_ref, weight_edge_ref,
        edge_ref, next_ref, normed_ref,
    ):
        gain_out, gain_in = upright(gain_out_ref[:1]), upright(gain_in_ref[1:])
        weight_out, weight_edge = weight_out_ref[0].T, halved(weight_edge_ref[1])
        for first in range(0, cols, GROUP):
            values = product_ref[:, first : first + GROUP].astype(f32).reshape(width, GROUP * rows)
            lefts, rights = [], []
            for step in range(0, GROUP, SUB):
                at = slice((first + step) * rows, (first + step + SUB) * rows)
                product = values[:, step * rows : (step + SUB) * rows]
                mixed = norm(product, gain_out, 0).astype(bf16)
                state = state_ref[:, at] + gate_ref[:, at] * dot(weight_out, mixed, (1, 0))
                next_ref[:, at] = state
                normed = norm(state, gain_in, 0).astype(bf16)
                normed_ref[:, at] = normed
                left, right = gated(dot(weight_edge, normed, (1, 0)), width)
                lefts.append(left)
                rights.append(right)
            put_edges(edge_ref, first, lefts, rights)

    shapes = [
        jax.ShapeDtypeStruct((width, 2, cols, rows), bf16),
        jax.ShapeDtypeStruct((width, cols * rows), f32),
        jax.ShapeDtypeStruct((width, cols * rows), bf16),
    ]
    return call(kernel, "middle", [VMEM] * 7, [VMEM] * 3, shapes)(
        product, gate, state, gains_out, weight_out, gains_in, weight_edge
    )


def second_gate(state, normed, weight, rows):
    width, pairs = state.shape

    def kernel(state_ref, normed_ref, weight_ref, gate_ref, turned_ref):
        for start in range(0, pairs, SUB * rows):
            at = slice(start, start + SUB * rows)
            gate_ref[at] = sigmoid(dot(normed_ref[:, at], weight_ref[1], (0, 0)))
            turned_ref[at] = state_ref[:, at].T

    shapes = [jax.ShapeDtypeStruct((pairs, width), f32)] * 2
    return call(kernel, "second_gate", [VMEM] * 3, [VMEM] * 2, shapes)(state, normed, weight)


def last(product, gate, state, gains, weight):
    width, cols, rows = product.shape
    chunk = 8

    def kernel(product_ref, gate_ref, state_ref, gain_ref, weight_ref, out_ref, held, sems):
        gain = upright(gain_ref[1:])
        written = []
        for first in range(0, cols, GROUP):
            values = product_ref[:, first : first + GROUP].astype(f32).reshape(width, GROUP * rows)
            for col in range(first, first + GROUP, SUB):
                at = slice(col * rows, (col + SUB) * rows)
                mixed = norm(values[:, (col - first) * rows : (col - first + SUB) * rows], gain, 0).astype(bf16)
                done = state_ref[at] + gate_ref[at] * dot(mixed, weight_ref[1], (0, 0))
                held[:, col : col + SUB] = jnp.swapaxes(done.reshape(SUB, rows, width), 0, 1)
                if (col + SUB) % chunk == 0:
                    ready = slice(col + SUB - chunk, col + SUB)
                    written.append(pltpu.make_async_copy(held.at[:, ready], out_ref.at[:, ready], sems.at[len(written)]))
                    written[-1].start()
        for copy in written:
            copy.wait()

    shape = (rows, cols, width)
    scratch = [pltpu.VMEM(shape, f32), pltpu.SemaphoreType.DMA((cols // chunk,))]
    return call(kernel, "last", [VMEM] * 5, HBM, pltpu.HBM(shape, f32), scratch)(product, gate, state, gains, weight)


chips = ("z_lo", "x", "y", "z_hi")
X, Y, Z_HI, Z_LO = 4, 4, 2, 4


def exchange(values):
    return lax.all_to_all(values, chips, 0, 0, tiled=True)


def swap(values):
    return lax.ppermute(values, "core", [(0, 1), (1, 0)])


def shards(state, gains_in, edge_weight, gate_weight, gains_out, out_weight):
    rows, cols, width = state.shape
    by_device = (X * Z_LO, Y * Z_HI, 2, cols, rows)
    core, gains_in = lax.optimization_barrier((lax.axis_index("core").astype(jnp.int32).reshape(1), gains_in))

    edge = exchange(first_edges(state, gains_in, edge_weight).reshape(width, 2 * cols, rows))
    own, send = outgoing(core, edge.reshape(by_device))
    sent = swap(send)
    gate, turned = first_gate(state, gains_in, gate_weight)
    product = add_partials(own, sent, Y * Z_HI, gate, turned)
    product = exchange(product.reshape(width, cols, rows))

    edge, state, normed = middle(product, gate, turned, gains_out, out_weight, gains_in, edge_weight)
    edge = exchange(edge.reshape(width, 2 * cols, rows)).reshape(by_device)
    sent = swap(edge[:, :, 0])
    gate, turned = second_gate(state, normed, gate_weight, rows)
    product = incoming(core, edge, sent, gate, turned)
    product = exchange(product.reshape(width, cols, rows))
    return last(product, gate, turned, gains_out, out_weight)


def solution(mesh):
    mesh = Mesh(mesh.devices.reshape(Z_HI, Y, X, Z_LO, 2), ("z_hi", "y", "x", "z_lo", "core"))
    placed = P(("z_hi", "y"), ("x", "z_lo", "core"), None)
    return jax.shard_map(
        shards,
        mesh=mesh,
        in_specs=(placed, P(), P(), P(), P(), P()),
        out_specs=placed,
        check_vma=False,
    )
```

```python
import jax
import jax.numpy as jnp
from jax import lax
from jax.experimental import pallas as pl
from jax.experimental.pallas import tpu as pltpu
from jax.sharding import Mesh
from jax.sharding import PartitionSpec as P

epsilon = 1e-05
bf16 = jnp.bfloat16
f32 = jnp.float32
GROUP = 16
SUB = 8
SHRINK = 2.0**-8


def norm(values, gain, axis):
    center = jnp.mean(values, axis=axis, keepdims=True)
    moved = values - center
    spread = jnp.mean(jnp.square(moved), axis=axis, keepdims=True)
    return moved * lax.rsqrt(spread + epsilon) * gain


def dot(a, b, contract):
    return lax.dot_general(a, b, ((contract[:1], contract[1:]), ((), ())), preferred_element_type=f32)


def sigmoid(values):
    return 0.5 * jnp.tanh(0.5 * values) + 0.5


def upright(row):
    return jnp.broadcast_to(row, (row.shape[1], row.shape[1])).T[:, :1]


def halved(weight):
    return (weight.astype(f32) * 0.5).T.astype(bf16)


def gated(projected, width):
    sides = [projected[n * width : (n + 1) * width] for n in range(4)]
    return jnp.tanh(sides[1]) * sides[0] + sides[0], jnp.tanh(sides[3]) * sides[2] + sides[2]


def put_edges(out_ref, at, lefts, rights):
    width, _, _, rows = out_ref.shape
    for side, parts in enumerate((lefts, rights)):
        values = jnp.concatenate(parts, axis=1)
        out_ref[:, side, at : at + GROUP] = values.reshape(width, GROUP, rows).astype(bf16)


VMEM = pl.BlockSpec(memory_space=pltpu.VMEM)
SMEM = pl.BlockSpec(memory_space=pltpu.SMEM)
HBM = pl.BlockSpec(memory_space=pltpu.HBM)
ANY = pl.BlockSpec(memory_space=pl.ANY)


def call(kernel, name, specs, outs, shapes, scratch=(), mib=16):
    return pl.pallas_call(
        kernel,
        in_specs=specs,
        out_specs=outs,
        out_shape=shapes,
        scratch_shapes=scratch,
        compiler_params=pltpu.CompilerParams(vmem_limit_bytes=mib << 20),
        name=name,
    )


def in_hbm(*values):
    return [pltpu.with_memory_space_constraint(value, pltpu.HBM) for value in values]


def start_all(copies):
    for copy in copies:
        copy.start()


def first_edges(state, gains, weight):
    rows, cols, width = state.shape
    chunk = 8

    def kernel(state_ref, gain_hbm, weight_hbm, out_ref, held, gain_ref, weight_ref, sems):
        whole = [
            pltpu.make_async_copy(gain_hbm, gain_ref, sems.at[0]),
            pltpu.make_async_copy(weight_hbm.at[0], weight_ref, sems.at[1]),
        ]
        parts = []
        for n in range(cols // chunk):
            at = slice(n * chunk, (n + 1) * chunk)
            parts.append(pltpu.make_async_copy(state_ref.at[:, at], held.at[:, at], sems.at[2 + n]))
        start_all(whole + parts)
        for copy in whole:
            copy.wait()
        turned = halved(weight_ref[...])
        for at in range(0, cols, GROUP):
            lefts, rights = [], []
            for col in range(at, at + GROUP, SUB):
                if col % chunk == 0:
                    parts[col // chunk].wait()
                values = jnp.swapaxes(held[:, col : col + SUB], 0, 1).reshape(SUB * rows, width)
                normed = norm(values, gain_ref[:1], 1).astype(bf16)
                left, right = gated(dot(turned, normed, (1, 1)), width)
                lefts.append(left)
                rights.append(right)
            put_edges(out_ref, at, lefts, rights)

    shape = jax.ShapeDtypeStruct((width, 2, cols, rows), bf16)
    scratch = [
        pltpu.VMEM((rows, cols, width), f32),
        pltpu.VMEM(gains.shape, f32),
        pltpu.VMEM(weight.shape[1:], bf16),
        pltpu.SemaphoreType.DMA((2 + cols // chunk,)),
    ]
    return call(kernel, "first_edges", [HBM] * 3, VMEM, shape, scratch)(*in_hbm(state, gains, weight))


def first_gate(state, gains, weight):
    rows, cols, width = state.shape

    def kernel(state_ref, gain_ref, weight_ref, gate_ref, turned_ref):
        for col in range(0, cols, SUB):
            values = jnp.swapaxes(state_ref[:, col : col + SUB], 0, 1).reshape(SUB * rows, width)
            normed = norm(values, gain_ref[:1], 1).astype(bf16)
            at = slice(col * rows, (col + SUB) * rows)
            gate_ref[:, at] = sigmoid(dot(weight_ref[0], normed, (0, 1)))
            turned_ref[:, at] = values.T

    shapes = [jax.ShapeDtypeStruct((width, cols * rows), f32)] * 2
    return call(kernel, "first_gate", [VMEM] * 3, [VMEM] * 2, shapes)(state, gains, weight)


def place_of(column_block):
    return column_block % Z_LO * X + column_block // Z_LO


def block_of(spot):
    return spot % Z_HI * Y + spot // Z_HI


def outgoing(core, edge):
    places, spots, _, cols, rows = edge.shape
    depth = places * cols
    per = rows // (2 * cols)

    def kernel(core_ref, edge_ref, own_ref, send_ref):
        mine = core_ref[0] == 0
        left = jnp.concatenate([edge_ref[:, spot, 0].reshape(depth, rows) for spot in range(spots)], axis=1)
        for spot in range(spots):
            right = edge_ref[:, spot, 1].reshape(depth, rows)
            partial = dot(right, left, (0, 0))
            for half in range(per):
                at = 2 * half * cols
                even, odd = partial[at : at + cols], partial[at + cols : at + 2 * cols]
                place = place_of(block_of(spot) * per + half)
                own_ref[place] = jnp.where(mine, even, odd)
                send_ref[place] = jnp.where(mine, odd, even)

    shapes = [jax.ShapeDtypeStruct((places, cols, spots * rows), f32)] * 2
    return call(kernel, "outgoing", [SMEM, VMEM], [VMEM] * 2, shapes)(core, edge)


def add_partials(own, other, spots, *made):
    places, cols, total = own.shape
    rows = total // spots

    def kernel(own_ref, other_ref, *refs):
        for spot in range(spots):
            at = slice(spot * rows, (spot + 1) * rows)
            refs[-1][:, spot] = (own_ref[:, :, at] + other_ref[:, :, at]) * SHRINK

    shape = jax.ShapeDtypeStruct((places, spots, cols, rows), f32)
    return call(kernel, "add_partials", [VMEM] * 2 + [ANY] * len(made), VMEM, shape)(own, other, *made)


def incoming(core, edge, other, *made):
    places, spots, _, cols, rows = edge.shape
    per = rows // (2 * cols)
    pair = 2

    def kernel(core_ref, edge_ref, other_ref, *refs):
        out_ref = refs[-1]
        mine = core_ref[0] == 0

        def left_of(place, side):
            parts = []
            for spot in range(spots):
                own, fetched = edge_ref[place, spot, 0], other_ref[place, spot]
                parts.append(jnp.where(mine, fetched, own) if side else jnp.where(mine, own, fetched))
            return jnp.concatenate(parts, axis=1)

        right = jnp.concatenate([edge_ref[:, spot, 1].reshape(places * cols, rows) for spot in range(spots)], axis=1)
        for first in range(0, spots, pair):
            left = jnp.concatenate(
                [
                    left_of(place_of(block_of(spot) * per + half), side)
                    for spot in range(first, first + pair)
                    for half in range(per)
                    for side in range(2)
                ],
                axis=0,
            )
            product = dot(right, left, (1, 1))
            for n in range(pair):
                at = slice(n * rows, (n + 1) * rows)
                out_ref[:, first + n] = product[:, at].reshape(places, cols, rows) * SHRINK

    shape = jax.ShapeDtypeStruct((places, spots, cols, rows), f32)
    specs = [SMEM, VMEM, VMEM] + [ANY] * len(made)
    return call(kernel, "incoming", specs, VMEM, shape)(core, edge, other, *made)


def middle(product, gate, state, gains_out, weight_out, gains_in, weight_edge):
    width, cols, rows = product.shape

    def kernel(
        product_ref, gate_ref, state_ref, gain_out_ref, weight_out_ref, gain_in_ref, weight_edge_ref,
        edge_ref, next_ref, normed_ref,
    ):
        gain_out, gain_in = upright(gain_out_ref[:1]), upright(gain_in_ref[1:])
        weight_out, weight_edge = weight_out_ref[0].T, halved(weight_edge_ref[1])
        for first in range(0, cols, GROUP):
            values = (product_ref[:, first : first + GROUP] * (1 / SHRINK)).reshape(width, GROUP * rows)
            lefts, rights = [], []
            for step in range(0, GROUP, SUB):
                at = slice((first + step) * rows, (first + step + SUB) * rows)
                product = values[:, step * rows : (step + SUB) * rows]
                mixed = norm(product, gain_out, 0).astype(bf16)
                state = state_ref[:, at] + gate_ref[:, at] * dot(weight_out, mixed, (1, 0))
                next_ref[:, at] = state
                normed = norm(state, gain_in, 0).astype(bf16)
                normed_ref[:, at] = normed
                left, right = gated(dot(weight_edge, normed, (1, 0)), width)
                lefts.append(left)
                rights.append(right)
            put_edges(edge_ref, first, lefts, rights)

    shapes = [
        jax.ShapeDtypeStruct((width, 2, cols, rows), bf16),
        jax.ShapeDtypeStruct((width, cols * rows), f32),
        jax.ShapeDtypeStruct((width, cols * rows), bf16),
    ]
    return call(kernel, "middle", [VMEM] * 7, [VMEM] * 3, shapes)(
        product, gate, state, gains_out, weight_out, gains_in, weight_edge
    )


def second_gate(state, normed, weight, rows):
    width, pairs = state.shape

    def kernel(state_ref, normed_ref, weight_ref, gate_ref, turned_ref):
        for start in range(0, pairs, SUB * rows):
            at = slice(start, start + SUB * rows)
            gate_ref[at] = sigmoid(dot(normed_ref[:, at], weight_ref[1], (0, 0)))
            turned_ref[at] = state_ref[:, at].T

    shapes = [jax.ShapeDtypeStruct((pairs, width), f32)] * 2
    return call(kernel, "second_gate", [VMEM] * 3, [VMEM] * 2, shapes)(state, normed, weight)


def last(product, gate, state, gains, weight):
    width, cols, rows = product.shape
    chunk = 8

    def kernel(product_ref, gate_ref, state_ref, gain_ref, weight_ref, out_ref, held, sems):
        gain = upright(gain_ref[1:])
        written = []
        for first in range(0, cols, GROUP):
            values = (product_ref[:, first : first + GROUP] * (1 / SHRINK)).reshape(width, GROUP * rows)
            for col in range(first, first + GROUP, SUB):
                at = slice(col * rows, (col + SUB) * rows)
                mixed = norm(values[:, (col - first) * rows : (col - first + SUB) * rows], gain, 0).astype(bf16)
                done = state_ref[at] + gate_ref[at] * dot(mixed, weight_ref[1], (0, 0))
                held[:, col : col + SUB] = jnp.swapaxes(done.reshape(SUB, rows, width), 0, 1)
                if (col + SUB) % chunk == 0:
                    ready = slice(col + SUB - chunk, col + SUB)
                    written.append(pltpu.make_async_copy(held.at[:, ready], out_ref.at[:, ready], sems.at[len(written)]))
                    written[-1].start()
        for copy in written:
            copy.wait()

    shape = (rows, cols, width)
    scratch = [pltpu.VMEM(shape, f32), pltpu.SemaphoreType.DMA((cols // chunk,))]
    return call(kernel, "last", [VMEM] * 5, HBM, pltpu.HBM(shape, f32), scratch)(product, gate, state, gains, weight)


chips = ("z_lo", "x", "y", "z_hi")
X, Y, Z_HI, Z_LO = 4, 4, 2, 4


def exchange(values):
    return lax.all_to_all(values, chips, 0, 0, tiled=True)


def swap(values):
    return lax.ppermute(values, "core", [(0, 1), (1, 0)])


def shards(state, gains_in, edge_weight, gate_weight, gains_out, out_weight):
    rows, cols, width = state.shape
    by_device = (X * Z_LO, Y * Z_HI, 2, cols, rows)
    core, gains_in = lax.optimization_barrier((lax.axis_index("core").astype(jnp.int32).reshape(1), gains_in))

    edge = exchange(first_edges(state, gains_in, edge_weight).reshape(width, 2 * cols, rows))
    own, send = outgoing(core, edge.reshape(by_device))
    sent = swap(send)
    gate, turned = first_gate(state, gains_in, gate_weight)
    product = add_partials(own, sent, Y * Z_HI, gate, turned)
    product = exchange(product.reshape(width, cols, rows).astype(jnp.float16)).astype(f32)

    edge, state, normed = middle(product, gate, turned, gains_out, out_weight, gains_in, edge_weight)
    edge = exchange(edge.reshape(width, 2 * cols, rows)).reshape(by_device)
    sent = swap(edge[:, :, 0])
    gate, turned = second_gate(state, normed, gate_weight, rows)
    product = incoming(core, edge, sent, gate, turned)
    product = exchange(product.reshape(width, cols, rows).astype(jnp.float16)).astype(f32)
    return last(product, gate, turned, gains_out, out_weight)


def solution(mesh):
    mesh = Mesh(mesh.devices.reshape(Z_HI, Y, X, Z_LO, 2), ("z_hi", "y", "x", "z_lo", "core"))
    placed = P(("z_hi", "y"), ("x", "z_lo", "core"), None)
    return jax.shard_map(
        shards,
        mesh=mesh,
        in_specs=(placed, P(), P(), P(), P(), P()),
        out_specs=placed,
        check_vma=False,
    )
```

```python
import jax
import jax.numpy as jnp
from jax import lax
from jax.experimental import pallas as pl
from jax.experimental.pallas import tpu as pltpu
from jax.sharding import Mesh
from jax.sharding import PartitionSpec as P

epsilon = 1e-05
bf16 = jnp.bfloat16
f32 = jnp.float32
GROUP = 16
SUB = 8


def norm(values, gain, axis):
    center = jnp.mean(values, axis=axis, keepdims=True)
    moved = values - center
    spread = jnp.mean(jnp.square(moved), axis=axis, keepdims=True)
    return moved * lax.rsqrt(spread + epsilon) * gain


def dot(a, b, contract):
    return lax.dot_general(a, b, ((contract[:1], contract[1:]), ((), ())), preferred_element_type=f32)


def sigmoid(values):
    return 0.5 * jnp.tanh(0.5 * values) + 0.5


def upright(row):
    return jnp.broadcast_to(row, (row.shape[1], row.shape[1])).T[:, :1]


def halved(weight):
    return (weight.astype(f32) * 0.5).T.astype(bf16)


def gated(projected, width):
    sides = [projected[n * width : (n + 1) * width] for n in range(4)]
    return jnp.tanh(sides[1]) * sides[0] + sides[0], jnp.tanh(sides[3]) * sides[2] + sides[2]


def put_edges(out_ref, at, lefts, rights):
    width, _, _, rows = out_ref.shape
    for side, parts in enumerate((lefts, rights)):
        values = jnp.concatenate(parts, axis=1)
        out_ref[:, side, at : at + GROUP] = values.reshape(width, GROUP, rows).astype(bf16)


VMEM = pl.BlockSpec(memory_space=pltpu.VMEM)
SMEM = pl.BlockSpec(memory_space=pltpu.SMEM)
HBM = pl.BlockSpec(memory_space=pltpu.HBM)
ANY = pl.BlockSpec(memory_space=pl.ANY)


def call(kernel, name, specs, outs, shapes, scratch=(), mib=16):
    return pl.pallas_call(
        kernel,
        in_specs=specs,
        out_specs=outs,
        out_shape=shapes,
        scratch_shapes=scratch,
        compiler_params=pltpu.CompilerParams(vmem_limit_bytes=mib << 20),
        name=name,
    )


def in_hbm(*values):
    return [pltpu.with_memory_space_constraint(value, pltpu.HBM) for value in values]


def start_all(copies):
    for copy in copies:
        copy.start()


def first_edges(state, gains, weight):
    rows, cols, width = state.shape
    chunk = 8

    def kernel(state_ref, gain_hbm, weight_hbm, out_ref, held, gain_ref, weight_ref, sems):
        whole = [
            pltpu.make_async_copy(gain_hbm, gain_ref, sems.at[0]),
            pltpu.make_async_copy(weight_hbm.at[0], weight_ref, sems.at[1]),
        ]
        parts = []
        for n in range(cols // chunk):
            at = slice(n * chunk, (n + 1) * chunk)
            parts.append(pltpu.make_async_copy(state_ref.at[:, at], held.at[:, at], sems.at[2 + n]))
        start_all(whole + parts)
        for copy in whole:
            copy.wait()
        turned = halved(weight_ref[...])
        for at in range(0, cols, GROUP):
            lefts, rights = [], []
            for col in range(at, at + GROUP, SUB):
                if col % chunk == 0:
                    parts[col // chunk].wait()
                values = jnp.swapaxes(held[:, col : col + SUB], 0, 1).reshape(SUB * rows, width)
                normed = norm(values, gain_ref[:1], 1).astype(bf16)
                left, right = gated(dot(turned, normed, (1, 1)), width)
                lefts.append(left)
                rights.append(right)
            put_edges(out_ref, at, lefts, rights)

    shape = jax.ShapeDtypeStruct((width, 2, cols, rows), bf16)
    scratch = [
        pltpu.VMEM((rows, cols, width), f32),
        pltpu.VMEM(gains.shape, f32),
        pltpu.VMEM(weight.shape[1:], bf16),
        pltpu.SemaphoreType.DMA((2 + cols // chunk,)),
    ]
    return call(kernel, "first_edges", [HBM] * 3, VMEM, shape, scratch)(*in_hbm(state, gains, weight))


def first_gate(state, gains, weight):
    rows, cols, width = state.shape

    def kernel(state_ref, gain_ref, weight_ref, gate_ref, turned_ref):
        for col in range(0, cols, SUB):
            values = jnp.swapaxes(state_ref[:, col : col + SUB], 0, 1).reshape(SUB * rows, width)
            normed = norm(values, gain_ref[:1], 1).astype(bf16)
            at = slice(col * rows, (col + SUB) * rows)
            gate_ref[:, at] = sigmoid(dot(weight_ref[0], normed, (0, 1)))
            turned_ref[:, at] = values.T

    shapes = [jax.ShapeDtypeStruct((width, cols * rows), f32)] * 2
    return call(kernel, "first_gate", [VMEM] * 3, [VMEM] * 2, shapes)(state, gains, weight)


def place_of(column_block):
    return column_block % Z_LO * X + column_block // Z_LO


def block_of(spot):
    return spot % Z_HI * Y + spot // Z_HI


def outgoing(core, edge):
    places, spots, _, cols, rows = edge.shape
    depth = places * cols
    per = rows // (2 * cols)

    def kernel(core_ref, edge_ref, own_ref, send_ref):
        mine = core_ref[0] == 0
        left = jnp.concatenate([edge_ref[:, spot, 0].reshape(depth, rows) for spot in range(spots)], axis=1)
        for spot in range(spots):
            if spot % 2 == 0:
                right = jnp.concatenate([edge_ref[:, spot + n, 1].reshape(depth, rows) for n in range(2)], axis=1)
                sums = dot(right, left, (0, 0))
            partial = sums[spot % 2 * rows : (spot % 2 + 1) * rows]
            for half in range(per):
                at = 2 * half * cols
                even, odd = partial[at : at + cols], partial[at + cols : at + 2 * cols]
                place = place_of(block_of(spot) * per + half)
                own_ref[place] = jnp.where(mine, even, odd)
                send_ref[place] = jnp.where(mine, odd, even)

    shapes = [jax.ShapeDtypeStruct((places, cols, spots * rows), f32)] * 2
    return call(kernel, "outgoing", [SMEM, VMEM], [VMEM] * 2, shapes)(core, edge)


def add_partials(own, other, spots, *made):
    places, cols, total = own.shape
    rows = total // spots

    def kernel(own_ref, other_ref, *refs):
        for spot in range(spots):
            at = slice(spot * rows, (spot + 1) * rows)
            refs[-1][:, spot] = (own_ref[:, :, at] + other_ref[:, :, at]).astype(bf16)

    shape = jax.ShapeDtypeStruct((places, spots, cols, rows), bf16)
    return call(kernel, "add_partials", [VMEM] * 2 + [ANY] * len(made), VMEM, shape)(own, other, *made)


def incoming(core, edge, other, *made):
    places, spots, _, cols, rows = edge.shape
    per = rows // (2 * cols)
    pair = 2

    def kernel(core_ref, edge_ref, other_ref, *refs):
        out_ref = refs[-1]
        mine = core_ref[0] == 0

        def left_of(place, side):
            parts = []
            for spot in range(spots):
                own, fetched = edge_ref[place, spot, 0], other_ref[place, spot]
                parts.append(jnp.where(mine, fetched, own) if side else jnp.where(mine, own, fetched))
            return jnp.concatenate(parts, axis=1)

        right = jnp.concatenate([edge_ref[:, spot, 1].reshape(places * cols, rows) for spot in range(spots)], axis=1)
        for first in range(0, spots, pair):
            left = jnp.concatenate(
                [
                    left_of(place_of(block_of(spot) * per + half), side)
                    for spot in range(first, first + pair)
                    for half in range(per)
                    for side in range(2)
                ],
                axis=0,
            )
            product = dot(right, left, (1, 1))
            for n in range(pair):
                at = slice(n * rows, (n + 1) * rows)
                out_ref[:, first + n] = product[:, at].reshape(places, cols, rows).astype(bf16)

    shape = jax.ShapeDtypeStruct((places, spots, cols, rows), bf16)
    specs = [SMEM, VMEM, VMEM] + [ANY] * len(made)
    return call(kernel, "incoming", specs, VMEM, shape)(core, edge, other, *made)


def middle(product, gate, state, gains_out, weight_out, gains_in, weight_edge):
    width, cols, rows = product.shape

    def kernel(
        product_ref, gate_ref, state_ref, gain_out_ref, weight_out_ref, gain_in_ref, weight_edge_ref,
        edge_ref, next_ref,
    ):
        gain_out, gain_in = upright(gain_out_ref[:1]), upright(gain_in_ref[1:])
        weight_out, weight_edge = weight_out_ref[0].T, halved(weight_edge_ref[1])
        for first in range(0, cols, GROUP):
            values = product_ref[:, first : first + GROUP].astype(f32).reshape(width, GROUP * rows)
            lefts, rights = [], []
            for step in range(0, GROUP, SUB):
                at = slice((first + step) * rows, (first + step + SUB) * rows)
                product = values[:, step * rows : (step + SUB) * rows]
                mixed = norm(product, gain_out, 0).astype(bf16)
                state = state_ref[:, at] + gate_ref[:, at] * dot(weight_out, mixed, (1, 0))
                next_ref[:, at] = state
                normed = norm(state, gain_in, 0).astype(bf16)
                left, right = gated(dot(weight_edge, normed, (1, 0)), width)
                lefts.append(left)
                rights.append(right)
            put_edges(edge_ref, first, lefts, rights)

    shapes = [
        jax.ShapeDtypeStruct((width, 2, cols, rows), bf16),
        jax.ShapeDtypeStruct((width, cols * rows), f32),
    ]
    return call(kernel, "middle", [VMEM] * 7, [VMEM] * 2, shapes)(
        product, gate, state, gains_out, weight_out, gains_in, weight_edge
    )


def second_gate(state, gains, weight, rows):
    width, pairs = state.shape

    def kernel(state_ref, gain_ref, weight_ref, gate_ref, turned_ref):
        gain = upright(gain_ref[1:])
        for start in range(0, pairs, SUB * rows):
            at = slice(start, start + SUB * rows)
            normed = norm(state_ref[:, at], gain, 0).astype(bf16)
            gate_ref[at] = sigmoid(dot(normed, weight_ref[1], (0, 0)))
            turned_ref[at] = state_ref[:, at].T

    shapes = [jax.ShapeDtypeStruct((pairs, width), f32)] * 2
    return call(kernel, "second_gate", [VMEM] * 3, [VMEM] * 2, shapes)(state, gains, weight)


def last(product, gate, state, gains, weight):
    width, cols, rows = product.shape
    chunk = 8

    def kernel(product_ref, gate_ref, state_ref, gain_ref, weight_ref, out_ref, held, sems):
        gain = upright(gain_ref[1:])
        written = []
        for first in range(0, cols, GROUP):
            values = product_ref[:, first : first + GROUP].astype(f32).reshape(width, GROUP * rows)
            for col in range(first, first + GROUP, SUB):
                at = slice(col * rows, (col + SUB) * rows)
                mixed = norm(values[:, (col - first) * rows : (col - first + SUB) * rows], gain, 0).astype(bf16)
                done = state_ref[at] + gate_ref[at] * dot(mixed, weight_ref[1], (0, 0))
                held[:, col : col + SUB] = jnp.swapaxes(done.reshape(SUB, rows, width), 0, 1)
                if (col + SUB) % chunk == 0:
                    ready = slice(col + SUB - chunk, col + SUB)
                    written.append(pltpu.make_async_copy(held.at[:, ready], out_ref.at[:, ready], sems.at[len(written)]))
                    written[-1].start()
        for copy in written:
            copy.wait()

    shape = (rows, cols, width)
    scratch = [pltpu.VMEM(shape, f32), pltpu.SemaphoreType.DMA((cols // chunk,))]
    return call(kernel, "last", [VMEM] * 5, HBM, pltpu.HBM(shape, f32), scratch)(product, gate, state, gains, weight)


chips = ("z_lo", "x", "y", "z_hi")
X, Y, Z_HI, Z_LO = 4, 4, 2, 4


def exchange(values):
    return lax.all_to_all(values, chips, 0, 0, tiled=True)


def swap(values):
    return lax.ppermute(values, "core", [(0, 1), (1, 0)])


def shards(state, gains_in, edge_weight, gate_weight, gains_out, out_weight):
    rows, cols, width = state.shape
    by_device = (X * Z_LO, Y * Z_HI, 2, cols, rows)
    core, gains_in = lax.optimization_barrier((lax.axis_index("core").astype(jnp.int32).reshape(1), gains_in))

    edge = exchange(first_edges(state, gains_in, edge_weight).reshape(width, 2 * cols, rows))
    own, send = outgoing(core, edge.reshape(by_device))
    sent = swap(send)
    gate, turned = first_gate(state, gains_in, gate_weight)
    product = add_partials(own, sent, Y * Z_HI, gate, turned)
    product = exchange(product.reshape(width, cols, rows))

    edge, state = middle(product, gate, turned, gains_out, out_weight, gains_in, edge_weight)
    edge = exchange(edge.reshape(width, 2 * cols, rows)).reshape(by_device)
    sent = swap(edge[:, :, 0])
    gate, turned = second_gate(state, gains_in, gate_weight, rows)
    product = incoming(core, edge, sent, gate, turned)
    product = exchange(product.reshape(width, cols, rows))
    return last(product, gate, turned, gains_out, out_weight)


def solution(mesh):
    mesh = Mesh(mesh.devices.reshape(Z_HI, Y, X, Z_LO, 2), ("z_hi", "y", "x", "z_lo", "core"))
    placed = P(("z_hi", "y"), ("x", "z_lo", "core"), None)
    return jax.shard_map(
        shards,
        mesh=mesh,
        in_specs=(placed, P(), P(), P(), P(), P()),
        out_specs=placed,
        check_vma=False,
    )
```
